32 devices in a mesh: groups: 2 (over y), rank: 4 (over z), tensor: 4 (over x, core).
Axes of the slice: x: 2, y: 2, z: 4, core: 2. Of those that a mesh axis runs over, the one named last changes fastest.
Arguments:
- tokens: bfloat16 [1024, 2048], P(('groups', 'rank'), 'tensor'), parts along dimension 0, may hold values from -6 to 6
- out_grad: bfloat16 [1024, 2048], P(('groups', 'rank'), 'tensor'), parts along dimension 0, may hold values from -0.3125 to 0.3125
- context: bfloat16 [1024, 2048], P(('groups', 'rank')), parts along dimension 0, may hold values from -6 to 6
- expert_ids: int32 [1024, 2], P(('groups', 'rank')), parts along dimension 0, may hold values from 0 to 7, all different within a row; in each aligned block of 128 rows (0 to 127, 128 to 255, ...) at most 40 rows name the same one
- gate_probs: bfloat16 [1024, 2], P(('groups', 'rank')), parts along dimension 0, may hold values from 0.19921875 to 1
- gate_weight: bfloat16 [2048, 57344], P(None, ('rank', 'tensor')), may hold values from -0.125 to 0.125
- up_weight: bfloat16 [2048, 57344], P(None, ('rank', 'tensor')), may hold values from -0.125 to 0.125
- down_weight: bfloat16 [57344, 2048], P('rank', 'tensor'), may hold values from -0.0625 to 0.0625
- kept_rows: int32 [16, 128], P('tensor'), may hold values from 0 to 2047, as said below
Outputs:
- layer_output: bfloat16 [1024, 2048], P(('groups', 'rank'), 'tensor'), parts along dimension 0
- router_grad: float32 [1024, 2], P(('groups', 'rank')), parts along dimension 0
- masked_grad: float32 [32, 128, 128], P(('groups', 'tensor')), parts along dimension 0
The draws below stay inside these ranges and needn't reach their ends.
There are 2 independent parts, one for each index of `groups`. The reference program is written for one: setup_inputs(seed, part) draws one part's arguments, and reference() takes and returns one part's arrays. A program takes and returns all parts, laid end to end along the dimension named above; an argument that names none is the same for every part. Nothing has to cross between parts.
Inputs may be any that keep to these rules, and one draw needn't show every extreme that they name: `expert_ids`: each row names 2 different experts. Among the rows of one attention replica (aligned blocks of 128 rows) no expert is named more than 40 times, and in every draw some expert is named exactly 40 times in some block. `kept_rows`: row c holds 128 increasing row indices, one in each group of 16 consecutive rows; the same indices serve every replica.
All inputs are finite; a program needn't handle non-finite values.
Results may differ from the reference program's by a relative error of at most 0.0051.
Values may be sent and summed in bfloat16 or wider, within the bound.
No kernel may reach another device: no remote copies, remote signals or barrier semaphores. Data moves between devices by JAX's collectives and lax.ppermute only.
A program may use at most 192 MiB of HBM per device.

```python
import math
import jax
import jax.numpy as jnp
import numpy as np
from jax import lax

D = 2048
FF = 7168
EXPERTS = 8
TOP = 2
TOK_DEV = 128
MOST = 40
TOKENS = 512
UNITS = 57344
N_RANK = 4


def draw_kept_rows(key, part):
    key = jax.random.fold_in(key, 11)
    offsets = jax.random.randint(key, (D // 128, D // 16), 0, 16, dtype=jnp.int32)
    offsets = offsets.at[0, 0].set(0)
    offsets = offsets.at[D // 128 - 1, D // 16 - 1].set(15)
    starts = jnp.arange(D // 16, dtype=jnp.int32) * 16
    return (starts[None, :] + offsets).astype(jnp.int32)


def block_levels(key, extent, cuts, low, high):
    loudness = 1.0
    for dim, shards_of in cuts:
        draws = jax.random.uniform(jax.random.fold_in(jax.random.fold_in(key, 6), dim), (shards_of,), jnp.float32, low / len(cuts), high / len(cuts))
        loudness = loudness * jnp.repeat(jnp.exp(draws), extent[dim] // shards_of).reshape((-1,) + (1,) * (len(extent) - 1 - dim))
    return loudness


def routed_block(key, own, number, rows, amount, top, bound, slope):
    order = jax.random.permutation(key, amount)
    packed, usual = shares(amount, rows * top, bound, slope, True), shares(amount, rows * top, bound, slope, False)
    places = jnp.arange(amount)

    def named(tallies, turn):
        used = int((tallies > 0).sum())
        fixed = max(1, used // 4)
        passed = fixed + (places - fixed + turn * (used - fixed)) % max(1, amount - fixed)
        return jnp.zeros((amount,), jnp.int32).at[order[jnp.where(places < fixed, places, passed)]].set(jnp.asarray(tallies, jnp.int32))

    tallies = jnp.where(number % 4 == 0, named(packed, number // 4), named(usual, number - number // 4 - 1))
    mixed = jax.random.permutation(jax.random.fold_in(own, 3), amount)
    giver, sink = mixed[0:amount // 2 * 2:2], mixed[1:amount // 2 * 2:2]
    room = jnp.minimum(tallies[giver] - 1, bound - tallies[sink]) // 2
    room = jnp.where((giver == order[0]) | (sink == order[0]) | (tallies[sink] == 0), 0, jnp.maximum(room, 0))
    passed = jax.random.randint(jax.random.fold_in(own, 4), (amount // 2,), 0, 1 << 20) % (room + 1)
    tallies = tallies.at[giver].add(-passed).at[sink].add(passed)
    items = jnp.searchsorted(jnp.cumsum(tallies), jnp.arange(rows * top), side="right").astype(jnp.int32)
    listing = items.reshape(top, rows).T
    listing = listing[jax.random.permutation(jax.random.fold_in(own, 1), rows)]
    turn = jax.random.randint(jax.random.fold_in(own, 2), (rows, 1), 0, top)
    return jnp.take_along_axis(listing, (jnp.arange(top)[None, :] + turn) % top, axis=1)


def shares(amount, total, bound, skew, full):
    loads = [(1 << 20) // math.isqrt(grade ** skew) + 1 for grade in range(1, amount + 1)]
    largest = bound if full else min(bound, max(-(-total // amount), total * loads[0] // sum(loads)))
    least = 1 if total - largest >= amount - 1 else 0
    holding, spare = [largest] + [least] * (amount - 1), total - largest - least * (amount - 1)
    while spare > 0:
        movable = [i for i in range(1, amount) if holding[i] < largest] or [i for i in range(1, amount) if holding[i] < bound]
        mass, budget = sum([loads[i] for i in movable]), spare
        for i in movable:
            addition = min(bound - holding[i], max(1, budget * loads[i] // mass), spare)
            holding[i] = holding[i] + addition
            spare = spare - addition
    return np.array(holding)


def scatter_about(own_key, extent, width, bound, pieces=(), kind=jnp.bfloat16):
    drawn = width * jax.random.normal(own_key, extent, jnp.float32)
    if pieces:
        drawn = drawn * block_levels(own_key, extent, pieces, -0.22, 0.18)
    return jnp.clip(drawn, -bound, bound).astype(kind)


def setup_inputs(seed: int = 0, part: int = 0) -> dict:
    keys = jax.random.split(jax.random.key(seed), 10)
    part_keys = jax.random.split(jax.random.fold_in(keys[9], part), 10)
    tokens = scatter_about(part_keys[0], (TOKENS, D), 1.0, 6.0, ((0, 4), (1, 4)))
    out_grad = scatter_about(part_keys[1], (TOKENS, D), (D ** -0.5), 0.3125, ((0, 4), (1, 4)))
    context = scatter_about(part_keys[2], (TOKENS, D), (D ** 0.5 * TOKENS ** -0.5), 6.0, ((0, 4),))
    expert_ids_keys = jax.random.split(jax.random.fold_in(part_keys[3], 1), TOKENS // TOK_DEV)
    expert_ids_turns = jax.random.permutation(jax.random.fold_in(part_keys[3], 3), TOKENS // TOK_DEV)
    expert_ids = jax.vmap(lambda own, number: routed_block(jax.random.fold_in(part_keys[3], 2), own, number, TOK_DEV, EXPERTS, TOP, MOST, 2))(expert_ids_keys, expert_ids_turns).reshape((TOKENS, TOP))
    gate_probs = jnp.clip(0.19921875 + 0.80078125 * jax.random.uniform(part_keys[4], (TOKENS, TOP), jnp.float32) ** block_levels(part_keys[4], (TOKENS, TOP), ((0, 4),), -0.2, 0.2), 0.19921875, 1.0).astype(jnp.bfloat16)
    gate_weight = scatter_about(keys[5], (D, UNITS), D ** -0.5, 0.125, ((1, 16),))
    up_weight = scatter_about(keys[6], (D, UNITS), D ** -0.5, 0.125, ((1, 16),))
    down_weight = scatter_about(keys[7], (UNITS, D), FF ** -0.5, 0.0625, ((0, 4), (1, 4)))
    kept_rows = draw_kept_rows(jax.random.fold_in(keys[9], 71), part)
    return dict(tokens=tokens, out_grad=out_grad, context=context, expert_ids=expert_ids, gate_probs=gate_probs, gate_weight=gate_weight, up_weight=up_weight, down_weight=down_weight, kept_rows=kept_rows)


def reference(tokens, out_grad, context, expert_ids, gate_probs, gate_weight, up_weight, down_weight, kept_rows):
    capacity = MOST * N_RANK
    token_index = jnp.arange(TOKENS, dtype=jnp.int32)

    def add_expert(expert, totals):
        summed, router = totals
        matches = expert_ids == expert
        member = jnp.any(matches, axis=1)
        weight = jnp.sum(jnp.where(matches, gate_probs.astype(jnp.float32), 0.0), axis=1)
        position = (jnp.cumsum(member.astype(jnp.int32)) - 1).astype(jnp.int32)
        slot_ids = jnp.where(member, position, capacity).astype(jnp.int32)
        row_index = jnp.zeros((capacity,), jnp.int32).at[slot_ids].set(token_index, mode="drop")
        filled = jnp.zeros((capacity,), jnp.float32).at[slot_ids].set(1.0, mode="drop")
        routed_rows = tokens[row_index]
        offset = (expert * FF).astype(jnp.int32)
        gate_act = jnp.dot(routed_rows, lax.dynamic_slice_in_dim(gate_weight, offset, FF, 1), preferred_element_type=jnp.float32)
        up_act = jnp.dot(routed_rows, lax.dynamic_slice_in_dim(up_weight, offset, FF, 1), preferred_element_type=jnp.float32)
        hidden = (jax.nn.silu(gate_act) * up_act).astype(jnp.bfloat16)
        expert_out = jnp.dot(hidden, lax.dynamic_slice_in_dim(down_weight, offset, FF, 0), preferred_element_type=jnp.float32)
        expert_out = expert_out * filled[:, None]
        summed = summed.at[row_index].add(expert_out * weight[row_index][:, None])
        scores = jnp.sum(out_grad[row_index].astype(jnp.float32) * expert_out, axis=1)
        per_token = jnp.zeros((TOKENS,), jnp.float32).at[row_index].add(scores)
        router = router + jnp.where(matches, per_token[:, None], 0.0)
        return summed, router

    start_sum = jnp.zeros((TOKENS, D), jnp.float32)
    start_router = jnp.zeros((TOKENS, TOP), jnp.float32)
    summed, router = lax.fori_loop(0, EXPERTS, add_expert, (start_sum, start_router))

    grads = []
    for column in range(D // 128):
        picked = jnp.take(context, kept_rows[column], axis=1)
        grad_block = out_grad[:, column * 128:(column + 1) * 128]
        grads.append(jnp.dot(picked.T, grad_block, preferred_element_type=jnp.float32))
    masked_grad = jnp.stack(grads)
    return (summed.astype(jnp.bfloat16), router, masked_grad)
```

```python
import functools
import jax
import jax.numpy as jnp
from jax import lax
from jax.experimental import pallas as pl
from jax.experimental.pallas import tpu as pltpu
from jax.sharding import PartitionSpec as P

FF = 7168
MOST = 40


def route_tables(expert_ids, gate_probs, rank_count, rank_units, per_rank, capacity):
    token_count = expert_ids.shape[0]
    owners = jnp.arange(rank_count, dtype=jnp.int32)
    first_expert = owners * rank_units // FF
    served = first_expert[:, None] + jnp.arange(per_rank, dtype=jnp.int32)[None, :]
    matches = expert_ids[None, :, None, :] == served[:, None, :, None]
    zero_weight = jnp.zeros((), jnp.bfloat16)
    weights = jnp.sum(jnp.where(matches, gate_probs[None, :, None, :], zero_weight), axis=3)
    member = jnp.any(matches, axis=(2, 3))
    position = jnp.cumsum(member.astype(jnp.int32), axis=1) - 1
    slot_ids = jnp.arange(capacity, dtype=jnp.int32)
    picked = member[:, None, :] & (position[:, None, :] == slot_ids[None, :, None])
    token_index = jnp.arange(token_count, dtype=jnp.int32)
    row_index = jnp.sum(jnp.where(picked, token_index[None, None, :], 0), axis=2)
    filled = jnp.any(picked, axis=2)
    slot_weight = jnp.where(filled[:, :, None], weights[owners[:, None], row_index], zero_weight)
    return (matches, row_index, filled, slot_weight)


def shards(
    tokens,
    out_grad,
    context,
    expert_ids,
    gate_probs,
    gate_weight,
    up_weight,
    down_weight,
    kept_rows,
):
    rank_count = lax.axis_size("rank")
    tensor_count = lax.axis_size("tensor")
    dev_units = gate_weight.shape[1]
    rank_units = dev_units * tensor_count
    per_rank = max(1, rank_units // FF)
    unit_span = min(rank_units, FF)
    token_count = tokens.shape[0]
    column_count = tokens.shape[1]
    capacity = min(MOST * per_rank, token_count)
    zero_value = jnp.zeros((), jnp.bfloat16)
    matches, row_index, filled, slot_weight = route_tables(
        expert_ids, gate_probs, rank_count, rank_units, per_rank, capacity
    )
    grad_send = jnp.where(filled[:, :, None], out_grad[row_index], zero_value)
    whole_rows = lax.all_gather(tokens, "tensor", axis=1, tiled=True)
    token_send = jnp.where(filled[:, :, None], whole_rows[row_index], zero_value)
    flat_index = row_index.reshape(-1)
    owner_rows = jnp.arange(rank_count, dtype=jnp.int32)[:, None]
    received = (
        lax.all_to_all(token_send, "rank", split_axis=0, concat_axis=0, tiled=True),
        lax.all_to_all(grad_send, "rank", split_axis=0, concat_axis=0, tiled=True),
        lax.all_to_all(slot_weight, "rank", split_axis=0, concat_axis=0, tiled=True),
    )
    routed_rows = received[0]
    source_count = routed_rows.shape[0]
    item_count = routed_rows.shape[1]
    row_count = source_count * item_count
    token_rows = routed_rows.reshape(row_count, routed_rows.shape[2])
    gate_act = jnp.dot(token_rows, gate_weight, preferred_element_type=jnp.float32)
    up_act = jnp.dot(token_rows, up_weight, preferred_element_type=jnp.float32)
    hidden = (jax.nn.silu(gate_act) * up_act).astype(jnp.bfloat16)

    def add_units(totals, shard_piece):
        width = shard_piece.shape[1]
        if per_rank == 1:
            return (
                totals + jnp.dot(shard_piece, down_weight, preferred_element_type=jnp.float32)[None]
            )
        unit_index = jnp.arange(width, dtype=jnp.int32)
        products = []
        for which in range(per_rank):
            inside = (unit_index // unit_span == which)[None, :]
            masked_piece = jnp.where(inside, shard_piece, zero_value)
            products.append(jnp.dot(masked_piece, down_weight, preferred_element_type=jnp.float32))
        return totals + jnp.stack(products)

    zero_out = jnp.zeros((per_rank, row_count, down_weight.shape[1]), jnp.float32)
    expert_out = add_units(zero_out, lax.all_gather(hidden, "tensor", axis=1, tiled=True))
    grad_flat = received[1].reshape(row_count, column_count).astype(jnp.float32)
    weight_flat = received[2].reshape(row_count, per_rank).astype(jnp.float32)
    output_part = jnp.sum(expert_out * jnp.transpose(weight_flat)[:, :, None], axis=0)
    router_part = jnp.transpose(jnp.sum(expert_out * grad_flat[None], axis=2))
    router_part = lax.psum(router_part, "tensor")
    output_back = lax.all_to_all(
        output_part.reshape(source_count, item_count, column_count),
        "rank",
        split_axis=0,
        concat_axis=0,
        tiled=True,
    )
    router_back = lax.all_to_all(
        router_part.reshape(source_count, item_count, per_rank),
        "rank",
        split_axis=0,
        concat_axis=0,
        tiled=True,
    )
    output_rows = jnp.where(filled[:, :, None], output_back, 0.0).reshape(-1, column_count)
    layer_sum = jnp.zeros((token_count, column_count), jnp.float32).at[flat_index].add(output_rows)
    layer_output = layer_sum.astype(jnp.bfloat16)
    router_terms = jnp.where(filled[:, :, None], router_back, 0.0)
    per_token = (
        jnp.zeros((rank_count, token_count, per_rank), jnp.float32)
        .at[owner_rows, row_index]
        .add(router_terms)
    )
    router_grad = jnp.sum(jnp.where(matches, per_token[:, :, :, None], 0.0), axis=(0, 2))
    local_blocks = kept_rows.shape[0]
    keep_count = kept_rows.shape[1]
    picked_context = jnp.take(context, kept_rows.reshape(-1), axis=1).reshape(
        token_count, local_blocks, keep_count
    )
    grad_blocks = out_grad.reshape(token_count, local_blocks, 128)
    local_grad = jnp.einsum(
        "tck,tcj->ckj", picked_context, grad_blocks, preferred_element_type=jnp.float32
    )
    masked_grad = lax.psum(local_grad, "rank")
    return (layer_output, router_grad, masked_grad)


OWNERS = 4
LISTS = 8
ROWS = OWNERS * MOST
CHUNKS = (512, 1024, 1024, 1024)
BLOCK = 256
DEEP = 512


def call(kernel, outs, name, *, flops=0, moved=0, grid=None, in_specs=None, out_specs=None, scratch=(), scalars=0):
    space = pltpu.PrefetchScalarGridSpec(
        num_scalar_prefetch=scalars,
        grid=grid or (),
        in_specs=in_specs,
        out_specs=out_specs,
        scratch_shapes=scratch,
    )
    return pl.pallas_call(
        kernel,
        out_shape=outs,
        grid_spec=space,
        name=name,
        compiler_params=pltpu.CompilerParams(vmem_limit_bytes=24 * 2**20),
        cost_estimate=pl.CostEstimate(flops=flops, bytes_accessed=moved, transcendentals=0),
    )


def whole():
    return pl.BlockSpec(memory_space=pltpu.VMEM)


def slot_codes(place, ids_ref):
    rank, chip = place[0], place[1] // 2
    count = ids_ref.shape[0]
    lists = lax.broadcasted_iota(jnp.int32, (LISTS, count), 0)
    experts = 2 * (rank ^ (lists // 2)) + (chip ^ (lists % 2))
    chosen = []
    for k in range(2):
        column = jnp.broadcast_to(ids_ref[:, k : k + 1].astype(jnp.float32), (count, count))
        chosen.append(jnp.transpose(column)[:LISTS].astype(jnp.int32) == experts)
    member = jnp.where(chosen[0] | chosen[1], 1.0, 0.0).astype(jnp.bfloat16)
    earlier = lax.broadcasted_iota(jnp.int32, (count, count), 0) < lax.broadcasted_iota(
        jnp.int32, (count, count), 1
    )
    before = jnp.where(earlier, 1.0, 0.0).astype(jnp.bfloat16)
    position = jnp.dot(member, before, preferred_element_type=jnp.float32)
    return [jnp.where(c, position, -1.0) for c in chosen]


def slot_matrix(code):
    count = code.shape[1]
    slots = lax.broadcasted_iota(jnp.int32, (MOST, count), 0).astype(jnp.float32)
    return jnp.concatenate(
        [jnp.where(code[q : q + 1] == slots, 1.0, 0.0) for q in range(LISTS)], axis=0
    )


def pack_kernel(place, ids_ref, tokens_ref, *out_refs):
    first, second = slot_codes(place, ids_ref)
    pick = slot_matrix(jnp.maximum(first, second)).astype(jnp.bfloat16)
    rows = jnp.dot(pick, tokens_ref[...], preferred_element_type=jnp.float32)
    for s in range(OWNERS):
        out_refs[s][...] = rows[2 * MOST * s : 2 * MOST * (s + 1)].astype(jnp.bfloat16)


def route_kernel(place, ids_ref, out_ref):
    count = ids_ref.shape[0]
    for k, code in enumerate(slot_codes(place, ids_ref)):
        pick = jnp.concatenate([slot_matrix(code), jnp.zeros((64, count), jnp.float32)], axis=0)
        out_ref[k] = jnp.transpose(pick).astype(jnp.bfloat16)


def split_kernel(*refs):
    own_ref, other_ref = refs[OWNERS:]
    order = [refs[s][...].astype(jnp.float32) for s in (1, 2, 3, 0)]
    own_ref[...] = jnp.concatenate([d[:MOST] for d in order], axis=0).astype(jnp.bfloat16)
    other_ref[...] = jnp.concatenate([d[MOST:] for d in order], axis=0).astype(jnp.bfloat16)


def hidden_kernel(place, a0, a1, a2, a3, gate_ref, up_ref, out_ref, rows):
    @pl.when(pl.program_id(0) == 0)
    def _():
        for j, piece in enumerate((a0, a1, a2, a3)):
            width = piece.shape[1]
            start = pl.multiple_of((place[1] ^ j) * width, width)
            rows[:, pl.ds(start, width)] = piece[...]

    gate = jnp.dot(rows[...], gate_ref[...], preferred_element_type=jnp.float32)
    up = jnp.dot(rows[...], up_ref[...], preferred_element_type=jnp.float32)
    out_ref[...] = (gate / (1.0 + jnp.exp(-gate)) * up).astype(jnp.bfloat16)


def hidden_chunk(place, pieces, gate_weight, up_weight, start, width):
    depth = gate_weight.shape[0]
    first = start // BLOCK
    weight = pl.BlockSpec((depth, BLOCK), lambda i, place: (0, first + i))
    return call(
        hidden_kernel,
        jax.ShapeDtypeStruct((ROWS, width), jnp.bfloat16),
        "hidden",
        grid=(width // BLOCK,),
        in_specs=[whole()] * 4 + [weight, weight],
        out_specs=pl.BlockSpec((ROWS, BLOCK), lambda i, place: (0, i)),
        scratch=[pltpu.VMEM((ROWS, depth), jnp.bfloat16)],
        scalars=1,
        flops=4 * ROWS * depth * width,
        moved=4 * depth * width,
    )(place, *pieces, gate_weight, up_weight)


def down_kernel(has_total, last, place, *refs):
    near, far, near_weight, far_weight = refs[:4]
    refs = refs[4:]
    total_in = None
    if has_total:
        total_in, refs = refs[0], refs[1:]
    outs, total = refs[:-1], refs[-1]
    step, steps = pl.program_id(0), pl.num_programs(0)
    part = jnp.dot(near[...], near_weight[...], preferred_element_type=jnp.float32) + jnp.dot(
        far[...], far_weight[...], preferred_element_type=jnp.float32
    )

    @pl.when(step == 0)
    def _():
        total[...] = part + total_in[...] if has_total else part

    @pl.when(step > 0)
    def _():
        total[...] += part

    @pl.when(step == steps - 1)
    def _():
        if last:
            for s in range(OWNERS):
                outs[s][...] = total[MOST * s : MOST * (s + 1), :].astype(jnp.bfloat16)
        else:
            outs[0][...] = total[...]


def down_chunk(place, near, far, down_weight, total, start, flip, last):
    width, columns = near.shape[1], down_weight.shape[1]
    half = FF // 2 // DEEP
    first = start // DEEP

    def block(core):
        return lambda i, place: (
            ((place[1] // 2) ^ flip) * 2 * half + ((place[1] % 2) ^ core) * half + first + i,
            0,
        )

    piece = pl.BlockSpec((ROWS, DEEP), lambda i, place: (0, i))
    in_specs = [piece, piece] + [pl.BlockSpec((DEEP, columns), block(core)) for core in (0, 1)]
    operands = [near, far, down_weight, down_weight]
    if total is not None:
        in_specs.append(whole())
        operands.append(total)
    if last:
        outs = [jax.ShapeDtypeStruct((MOST, columns), jnp.bfloat16)] * OWNERS
    else:
        outs = [jax.ShapeDtypeStruct((ROWS, columns), jnp.float32)]
    return call(
        functools.partial(down_kernel, total is not None, last),
        outs,
        "down",
        grid=(width // DEEP,),
        in_specs=in_specs,
        out_specs=[whole()] * len(outs),
        scratch=[pltpu.VMEM((ROWS, columns), jnp.float32)],
        scalars=1,
        flops=4 * ROWS * width * columns,
        moved=4 * width * columns,
    )(place, *operands)


def combine_kernel(*refs):
    lists, (route_ref, probs_ref, grad_ref, layer_ref, router_ref) = refs[:LISTS], refs[LISTS:]
    columns = grad_ref.shape[1]
    stacked = [ref[...].astype(jnp.float32) for ref in lists] + [jnp.zeros((64, columns), jnp.float32)]
    rows = jnp.concatenate(stacked, axis=0).astype(jnp.bfloat16)
    grad = grad_ref[...].astype(jnp.float32)
    probs = probs_ref[...].astype(jnp.float32)
    ones = jnp.ones((8, columns), jnp.float32)
    layer = None
    scores = []
    for k in range(2):
        chosen = jnp.dot(route_ref[k], rows, preferred_element_type=jnp.float32)
        term = probs[:, k : k + 1] * chosen
        layer = term if layer is None else layer + term
        scores.append(
            lax.dot_general(
                ones,
                grad * chosen,
                (((1,), (1,)), ((), ())),
                precision=lax.Precision.HIGHEST,
                preferred_element_type=jnp.float32,
            )
        )
    layer_ref[...] = layer.astype(jnp.bfloat16)
    line = lax.broadcasted_iota(jnp.int32, router_ref.shape, 0)
    router_ref[...] = jnp.where(line == 0, scores[0], scores[1])


def router_kernel(p0, p1, p2, p3, out_ref):
    total = (p0[...] + p1[...]) + (p2[...] + p3[...])
    square = jnp.concatenate([total] * 16, axis=0)
    out_ref[...] = jnp.transpose(square)[:, :2]


def masked_kernel(context_ref, grad_ref, kept_ref, out_ref):
    features, keep = context_ref.shape[1], kept_ref.shape[1]
    index = lax.broadcasted_iota(jnp.int32, (features, keep), 0)
    for c in range(kept_ref.shape[0]):
        pick = jnp.where(index == kept_ref[c : c + 1, :], 1.0, 0.0).astype(jnp.bfloat16)
        picked = jnp.dot(context_ref[...], pick, preferred_element_type=jnp.float32)
        part = lax.dot_general(
            picked.astype(jnp.bfloat16),
            grad_ref[:, 128 * c : 128 * (c + 1)],
            (((0,), (0,)), ((), ())),
            preferred_element_type=jnp.float32,
        )
        out_ref[c] = part.astype(jnp.bfloat16)


def add_kernel(p0, p1, p2, p3, out_ref):
    f32 = jnp.float32
    out_ref[...] = (p0[...].astype(f32) + p1[...].astype(f32)) + (p2[...].astype(f32) + p3[...].astype(f32))


def swap(value, axis, by):
    return lax.ppermute(value, axis, [(i, i ^ by) for i in range(4)])


def routed(
    tokens,
    out_grad,
    context,
    expert_ids,
    gate_probs,
    gate_weight,
    up_weight,
    down_weight,
    kept_rows,
):
    token_count, columns = tokens.shape
    bf16, f32 = jnp.bfloat16, jnp.float32
    shape = jax.ShapeDtypeStruct
    place = jnp.stack([lax.axis_index("rank"), lax.axis_index("tensor")]).astype(jnp.int32)
    packed = call(
        pack_kernel,
        [shape((2 * MOST, columns), bf16)] * OWNERS,
        "pack",
        in_specs=[whole()] * 2,
        out_specs=[whole()] * OWNERS,
        scalars=1,
    )(place, expert_ids, tokens)
    arrived = [packed[0]] + [swap(packed[s], "rank", s) for s in (1, 2, 3)]
    route = call(
        route_kernel,
        shape((2, token_count, 384), bf16),
        "route",
        in_specs=[whole()],
        out_specs=whole(),
        scalars=1,
    )(place, expert_ids)
    partial = call(
        masked_kernel,
        shape((kept_rows.shape[0], kept_rows.shape[1], 128), bf16),
        "masked",
        in_specs=[whole()] * 3,
        out_specs=whole(),
        flops=2 * context.shape[0] * context.shape[1] * 512,
        moved=2**20,
    )(context, out_grad, kept_rows)
    own, other = call(
        split_kernel,
        [shape((ROWS, columns), bf16)] * 2,
        "split",
        in_specs=[whole()] * OWNERS,
        out_specs=[whole()] * 2,
    )(*arrived)
    own_far = swap(own, "tensor", 1)
    crossed = swap(other, "tensor", 2)
    crossed_far = swap(crossed, "tensor", 1)
    pieces = (own, own_far, crossed, crossed_far)
    starts = [sum(CHUNKS[:i]) for i in range(len(CHUNKS))]
    hidden = [
        hidden_chunk(place, pieces, gate_weight, up_weight, start, width)
        for start, width in zip(starts, CHUNKS)
    ]
    partials = [partial] + [swap(partial, "rank", s) for s in (1, 2, 3)]
    masked_grad = call(
        add_kernel,
        shape(partial.shape, f32),
        "masked_sum",
        in_specs=[whole()] * 4,
        out_specs=whole(),
    )(*partials)
    across = [swap(h, "tensor", 2) for h in hidden]
    results = []
    for flip, parts in enumerate((hidden, across)):
        total = None
        for i, part in enumerate(parts):
            far = swap(part, "tensor", 1)
            last = i == len(parts) - 1
            outs = down_chunk(place, part, far, down_weight, total, starts[i], flip, last)
            total = outs[0]
        results.append([outs[3]] + [swap(outs[s - 1], "rank", s) for s in (1, 2, 3)])
    lists = [results[q % 2][q // 2] for q in range(LISTS)]
    layer_output, router = call(
        combine_kernel,
        [shape((token_count, columns), bf16), shape((8, token_count), f32)],
        "combine",
        in_specs=[whole()] * (LISTS + 3),
        out_specs=[whole()] * 2,
    )(*lists, route, gate_probs, out_grad)
    routers = [router] + [swap(router, "tensor", t) for t in (1, 2, 3)]
    router_grad = call(
        router_kernel,
        shape((token_count, 2), f32),
        "router",
        in_specs=[whole()] * 4,
        out_specs=whole(),
    )(*routers)
    return (layer_output, router_grad, masked_grad)


def solution(mesh):
    ranks, tensors = mesh.shape["rank"], mesh.shape["tensor"]
    body = routed if (ranks, tensors) == (4, 4) else shards
    return jax.shard_map(
        body,
        mesh=mesh,
        in_specs=(
            P(("groups", "rank"), "tensor"),
            P(("groups", "rank"), "tensor"),
            P(("groups", "rank"), None),
            P(("groups", "rank"), None),
            P(("groups", "rank"), None),
            P(None, ("rank", "tensor")),
            P(None, ("rank", "tensor")),
            P("rank", "tensor"),
            P("tensor", None),
        ),
        out_specs=(
            P(("groups", "rank"), "tensor"),
            P(("groups", "rank"), None),
            P(("groups", "tensor"), None, None),
        ),
        check_vma=False,
    )
```

```python
import functools
import jax
import jax.numpy as jnp
from jax import lax
from jax.experimental import pallas as pl
from jax.experimental.pallas import tpu as pltpu
from jax.sharding import PartitionSpec as P

FF = 7168
MOST = 40


def route_tables(expert_ids, gate_probs, rank_count, rank_units, per_rank, capacity):
    token_count = expert_ids.shape[0]
    owners = jnp.arange(rank_count, dtype=jnp.int32)
    first_expert = owners * rank_units // FF
    served = first_expert[:, None] + jnp.arange(per_rank, dtype=jnp.int32)[None, :]
    matches = expert_ids[None, :, None, :] == served[:, None, :, None]
    zero_weight = jnp.zeros((), jnp.bfloat16)
    weights = jnp.sum(jnp.where(matches, gate_probs[None, :, None, :], zero_weight), axis=3)
    member = jnp.any(matches, axis=(2, 3))
    position = jnp.cumsum(member.astype(jnp.int32), axis=1) - 1
    slot_ids = jnp.arange(capacity, dtype=jnp.int32)
    picked = member[:, None, :] & (position[:, None, :] == slot_ids[None, :, None])
    token_index = jnp.arange(token_count, dtype=jnp.int32)
    row_index = jnp.sum(jnp.where(picked, token_index[None, None, :], 0), axis=2)
    filled = jnp.any(picked, axis=2)
    slot_weight = jnp.where(filled[:, :, None], weights[owners[:, None], row_index], zero_weight)
    return (matches, row_index, filled, slot_weight)


def shards(
    tokens,
    out_grad,
    context,
    expert_ids,
    gate_probs,
    gate_weight,
    up_weight,
    down_weight,
    kept_rows,
):
    rank_count = lax.axis_size("rank")
    tensor_count = lax.axis_size("tensor")
    dev_units = gate_weight.shape[1]
    rank_units = dev_units * tensor_count
    per_rank = max(1, rank_units // FF)
    unit_span = min(rank_units, FF)
    token_count = tokens.shape[0]
    column_count = tokens.shape[1]
    capacity = min(MOST * per_rank, token_count)
    zero_value = jnp.zeros((), jnp.bfloat16)
    matches, row_index, filled, slot_weight = route_tables(
        expert_ids, gate_probs, rank_count, rank_units, per_rank, capacity
    )
    grad_send = jnp.where(filled[:, :, None], out_grad[row_index], zero_value)
    whole_rows = lax.all_gather(tokens, "tensor", axis=1, tiled=True)
    token_send = jnp.where(filled[:, :, None], whole_rows[row_index], zero_value)
    flat_index = row_index.reshape(-1)
    owner_rows = jnp.arange(rank_count, dtype=jnp.int32)[:, None]
    received = (
        lax.all_to_all(token_send, "rank", split_axis=0, concat_axis=0, tiled=True),
        lax.all_to_all(grad_send, "rank", split_axis=0, concat_axis=0, tiled=True),
        lax.all_to_all(slot_weight, "rank", split_axis=0, concat_axis=0, tiled=True),
    )
    routed_rows = received[0]
    source_count = routed_rows.shape[0]
    item_count = routed_rows.shape[1]
    row_count = source_count * item_count
    token_rows = routed_rows.reshape(row_count, routed_rows.shape[2])
    gate_act = jnp.dot(token_rows, gate_weight, preferred_element_type=jnp.float32)
    up_act = jnp.dot(token_rows, up_weight, preferred_element_type=jnp.float32)
    hidden = (jax.nn.silu(gate_act) * up_act).astype(jnp.bfloat16)

    def add_units(totals, shard_piece):
        width = shard_piece.shape[1]
        if per_rank == 1:
            return (
                totals + jnp.dot(shard_piece, down_weight, preferred_element_type=jnp.float32)[None]
            )
        unit_index = jnp.arange(width, dtype=jnp.int32)
        products = []
        for which in range(per_rank):
            inside = (unit_index // unit_span == which)[None, :]
            masked_piece = jnp.where(inside, shard_piece, zero_value)
            products.append(jnp.dot(masked_piece, down_weight, preferred_element_type=jnp.float32))
        return totals + jnp.stack(products)

    zero_out = jnp.zeros((per_rank, row_count, down_weight.shape[1]), jnp.float32)
    expert_out = add_units(zero_out, lax.all_gather(hidden, "tensor", axis=1, tiled=True))
    grad_flat = received[1].reshape(row_count, column_count).astype(jnp.float32)
    weight_flat = received[2].reshape(row_count, per_rank).astype(jnp.float32)
    output_part = jnp.sum(expert_out * jnp.transpose(weight_flat)[:, :, None], axis=0)
    router_part = jnp.transpose(jnp.sum(expert_out * grad_flat[None], axis=2))
    router_part = lax.psum(router_part, "tensor")
    output_back = lax.all_to_all(
        output_part.reshape(source_count, item_count, column_count),
        "rank",
        split_axis=0,
        concat_axis=0,
        tiled=True,
    )
    router_back = lax.all_to_all(
        router_part.reshape(source_count, item_count, per_rank),
        "rank",
        split_axis=0,
        concat_axis=0,
        tiled=True,
    )
    output_rows = jnp.where(filled[:, :, None], output_back, 0.0).reshape(-1, column_count)
    layer_sum = jnp.zeros((token_count, column_count), jnp.float32).at[flat_index].add(output_rows)
    layer_output = layer_sum.astype(jnp.bfloat16)
    router_terms = jnp.where(filled[:, :, None], router_back, 0.0)
    per_token = (
        jnp.zeros((rank_count, token_count, per_rank), jnp.float32)
        .at[owner_rows, row_index]
        .add(router_terms)
    )
    router_grad = jnp.sum(jnp.where(matches, per_token[:, :, :, None], 0.0), axis=(0, 2))
    local_blocks = kept_rows.shape[0]
    keep_count = kept_rows.shape[1]
    picked_context = jnp.take(context, kept_rows.reshape(-1), axis=1).reshape(
        token_count, local_blocks, keep_count
    )
    grad_blocks = out_grad.reshape(token_count, local_blocks, 128)
    local_grad = jnp.einsum(
        "tck,tcj->ckj", picked_context, grad_blocks, preferred_element_type=jnp.float32
    )
    masked_grad = lax.psum(local_grad, "rank")
    return (layer_output, router_grad, masked_grad)


OWNERS = 4
LISTS = 8
ROWS = OWNERS * MOST
REMOTE = ROWS - MOST
CHUNKS = (512, 896, 1024, 1152)
STARTS = (0, 512, 1408, 2432)
HALF = FF // 2
BLOCK = 256
PIECES = 4
LOADS = (((0, 0), (0, 1), (1, 0), (1, 1), (2, 0)), ((2, 1), (3, 0)), ((3, 1),))
ANY = pl.BlockSpec(memory_space=pl.ANY)
HBM = pl.BlockSpec(memory_space=pltpu.HBM)
VMEM = pl.BlockSpec(memory_space=pltpu.VMEM)


def call(kernel, name, operands, outs, *, after=(), far=(), scratch=(), aliases=None, cost=0):
    count, late = len(operands), len(after)
    operands = [
        pltpu.with_memory_space_constraint(x, pltpu.HBM) if i in far else x
        for i, x in enumerate(operands)
    ]

    def body(*refs):
        place = (lax.axis_index("rank"), lax.axis_index("tensor"))
        kernel(place, *refs[:count], *refs[count + late :])

    return pl.pallas_call(
        body,
        out_shape=outs,
        in_specs=[HBM if i in far else VMEM for i in range(count)] + [ANY] * late,
        out_specs=[VMEM] * len(outs),
        scratch_shapes=scratch,
        name=name,
        input_output_aliases=aliases or {},
        compiler_params=pltpu.CompilerParams(vmem_limit_bytes=8 * 2**20),
        cost_estimate=pl.CostEstimate(flops=0, bytes_accessed=int(cost * 3e6), transcendentals=0),
    )(*operands, *after)


def shape(*dims, dtype=jnp.bfloat16):
    return jax.ShapeDtypeStruct(dims, dtype)


def product(left, right):
    return jnp.dot(left, right, preferred_element_type=jnp.float32)


def slot_codes(place, ids_ref):
    rank, chip = place[0], place[1] // 2
    count = ids_ref.shape[1]
    lists = lax.broadcasted_iota(jnp.int32, (LISTS, count), 0)
    experts = 2 * (rank ^ (lists // 2)) + (chip ^ (lists % 2))
    chosen = [ids_ref[k : k + 1, :] == experts for k in range(2)]
    member = jnp.where(chosen[0] | chosen[1], 1.0, 0.0).astype(jnp.bfloat16)
    earlier = lax.broadcasted_iota(jnp.int32, (count, count), 0) < lax.broadcasted_iota(
        jnp.int32, (count, count), 1
    )
    before = jnp.where(earlier, 1.0, 0.0).astype(jnp.bfloat16)
    position = product(member, before)
    return [jnp.where(c, position, -1.0) for c in chosen]


def slot_matrix(code, value=1.0):
    count = code.shape[1]
    slots = lax.broadcasted_iota(jnp.int32, (MOST, count), 0).astype(jnp.float32)
    return jnp.concatenate(
        [jnp.where(code[q : q + 1] == slots, value, 0.0) for q in range(LISTS)], axis=0
    )


def pack_kernel(place, ids_ref, tokens_ref, *refs):
    outs, (ids, tokens, sems) = refs[:OWNERS], refs[OWNERS:]
    copies = [
        pltpu.make_async_copy(ids_ref, ids, sems.at[0]),
        pltpu.make_async_copy(tokens_ref, tokens, sems.at[1]),
    ]
    for copy in copies:
        copy.start()
    copies[0].wait()
    first, second = slot_codes(place, ids)
    pick = slot_matrix(jnp.maximum(first, second)).astype(jnp.bfloat16)
    copies[1].wait()
    rows = product(pick, tokens[...])
    for s in range(OWNERS):
        outs[s][...] = rows[2 * MOST * s : 2 * MOST * (s + 1)].astype(jnp.bfloat16)


def route_kernel(place, ids_ref, probs_ref, out_ref):
    count = ids_ref.shape[1]
    codes = slot_codes(place, ids_ref)
    probs = [probs_ref[k : k + 1, :].astype(jnp.float32) for k in range(2)]
    weighted = slot_matrix(codes[0], probs[0]) + slot_matrix(codes[1], probs[1])
    for k, pick in enumerate((slot_matrix(codes[0]), slot_matrix(codes[1]), weighted)):
        padded = jnp.concatenate([pick, jnp.zeros((64, count), jnp.float32)], axis=0)
        out_ref[k] = jnp.transpose(padded).astype(jnp.bfloat16)


def split_kernel(place, *refs):
    own_ref, other_ref = refs[OWNERS:]
    order = [refs[s][...].astype(jnp.float32) for s in (1, 2, 3, 0)]
    own_ref[...] = jnp.concatenate([d[:MOST] for d in order], axis=0).astype(jnp.bfloat16)
    other_ref[...] = jnp.concatenate([d[MOST:] for d in order], axis=0).astype(jnp.bfloat16)


def weight_copies(sources, outs, sems, load):
    copies = []
    for (chunk, which), out in zip(load, outs):
        part = out.shape[0] // PIECES
        for i in range(PIECES):
            rows = pl.ds(i * part, part)
            source = sources[which].at[rows, pl.ds(STARTS[chunk], CHUNKS[chunk])]
            copies.append(pltpu.make_async_copy(source, out.at[rows, :], sems.at[len(copies)]))
    return copies


def load_kernel(load, place, gate_ref, up_ref, *refs):
    copies = weight_copies((gate_ref, up_ref), refs[:-1], refs[-1], load)
    for copy in copies:
        copy.start()
    for copy in copies:
        copy.wait()


def masked_kernel(place, context_ref, grad_ref, kept_ref, gate_ref, up_ref, *refs):
    out_ref, weights, (context, grad, sems, few) = refs[0], refs[1:-4], refs[-4:]
    first = [
        pltpu.make_async_copy(context_ref, context, few.at[0]),
        pltpu.make_async_copy(grad_ref, grad, few.at[1]),
    ]
    copies = weight_copies((gate_ref, up_ref), weights, sems, LOADS[0])
    for copy in first + copies:
        copy.start()
    features, keep = context.shape[1], kept_ref.shape[1]
    index = lax.broadcasted_iota(jnp.int32, (features, keep), 0)
    for copy in first:
        copy.wait()
    for c in range(kept_ref.shape[0]):
        pick = jnp.where(index == kept_ref[c : c + 1, :], 1.0, 0.0).astype(jnp.bfloat16)
        picked = product(context[...], pick).astype(jnp.bfloat16)
        part = lax.dot_general(
            picked,
            grad[:, 128 * c : 128 * (c + 1)],
            (((0,), (0,)), ((), ())),
            preferred_element_type=jnp.float32,
        )
        out_ref[c] = part.astype(jnp.bfloat16)
    for copy in copies:
        copy.wait()


def pass_kernel(place, in_ref, out_ref):
    pass


def sum_kernel(place, left, right, out_ref):
    total = left[...].astype(jnp.float32) + right[...].astype(jnp.float32)
    out_ref[...] = total.astype(out_ref.dtype)


def hidden_kernel(place, a0, a1, a2, a3, gate_ref, up_ref, out_ref, remote_ref, rows):
    for j, piece in enumerate((a0, a1, a2, a3)):
        width = piece.shape[1]
        start = pl.multiple_of((place[1] ^ j) * width, width)
        rows[:, pl.ds(start, width)] = piece[...]
    for start in range(0, out_ref.shape[1], BLOCK):
        columns = slice(start, min(start + BLOCK, out_ref.shape[1]))
        gate = product(rows[...], gate_ref[:, columns])
        up = product(rows[...], up_ref[:, columns])
        hidden = gate / (1.0 + jnp.exp(-gate)) * up
        out_ref[:, columns] = hidden.astype(jnp.bfloat16)
        remote_ref[:, columns] = hidden[:REMOTE].astype(jnp.bfloat16)


def merge_kernel(place, *refs):
    for start, width, part in zip(STARTS, CHUNKS, refs):
        own = part[...].astype(jnp.float32)[REMOTE:]
        refs[-1][:, start : start + width] = own.astype(jnp.bfloat16)


def down_part(place, part, down_ref, start, flip, core):
    chip, own = (place[1] // 2) ^ flip, (place[1] % 2) ^ core
    rows = pl.ds(pl.multiple_of((2 * chip + own) * HALF + start, 128), part.shape[1])
    return product(part[...], down_ref[rows, :])


def down_own_kernel(place, *refs):
    parts, down_ref, outs = refs[: 2 * len(CHUNKS)], refs[2 * len(CHUNKS)], refs[2 * len(CHUNKS) + 1 :]
    total = None
    for i, part in enumerate(parts):
        term = down_part(place, part, down_ref, STARTS[i // 2], 0, i % 2)
        total = term if total is None else total + term
    for s in range(OWNERS):
        outs[s][...] = total[MOST * s : MOST * (s + 1)].astype(jnp.bfloat16)


def down_add_kernel(pieces, has_total, place, *refs):
    parts, down_ref, refs = refs[: len(pieces)], refs[len(pieces)], refs[len(pieces) + 1 :]
    total = refs[0][...] if has_total else None
    for (start, core), part in zip(pieces, parts):
        term = down_part(place, part, down_ref, start, 1, core)
        total = term if total is None else total + term
    refs[-1][...] = total


def back_kernel(place, total_ref, o1, o2, o3, *outs):
    total = total_ref[...]
    for s, own in enumerate((o1, o2, o3)):
        both = [own[...].astype(jnp.float32), total[MOST * s : MOST * (s + 1)]]
        outs[s][...] = jnp.concatenate(both, axis=0).astype(jnp.bfloat16)


def combine_kernel(place, own, other, b1, b2, b3, route_ref, grad_ref, layer_ref, router_ref):
    count, columns = grad_ref.shape
    stacked = [ref[...].astype(jnp.float32) for ref in (own, other, b1, b2, b3)]
    stacked.append(jnp.zeros((64, columns), jnp.float32))
    rows = jnp.concatenate(stacked, axis=0).astype(jnp.bfloat16)
    grad = grad_ref[...].astype(jnp.float32)
    layer_ref[...] = product(route_ref[2], rows).astype(jnp.bfloat16)
    lane = lax.broadcasted_iota(jnp.int32, (count, 128), 1)
    scores = jnp.zeros((count, 128), jnp.float32)
    for k in range(2):
        score = jnp.sum(grad * product(route_ref[k], rows), axis=1, keepdims=True)
        scores = jnp.where(lane == k, score, scores)
    router_ref[...] = jnp.transpose(scores)[:8]


def router_kernel(place, p0, p1, p2, p3, out_ref):
    out_ref[...] = ((p0[...] + p1[...]) + (p2[...] + p3[...]))[:2]


def swap(value, axis, by):
    return lax.ppermute(value, axis, [(i, i ^ by) for i in range(4)])


def routed(
    tokens,
    out_grad,
    context,
    expert_ids,
    gate_probs,
    gate_weight,
    up_weight,
    down_weight,
    kept_rows,
):
    token_count, columns = tokens.shape
    depth = gate_weight.shape[0]
    f32 = jnp.float32
    dma = pltpu.SemaphoreType.DMA
    ids, probs = expert_ids.T, gate_probs.T

    packed = call(
        pack_kernel,
        "pack",
        (ids, tokens),
        [shape(2 * MOST, columns)] * OWNERS,
        far=(0, 1),
        scratch=[pltpu.VMEM(ids.shape, ids.dtype), pltpu.VMEM(tokens.shape, tokens.dtype), dma((2,))],
    )
    arrived = [packed[0]] + [swap(packed[s], "rank", s) for s in (1, 2, 3)]
    weights = [[None, None] for _ in CHUNKS]

    def load(which, kernel, name, operands, outs, scratch, after):
        pieces = LOADS[which]
        shapes = [shape(depth, CHUNKS[chunk]) for chunk, _ in pieces]
        made = call(
            kernel,
            name,
            (*operands, gate_weight, up_weight),
            outs + shapes,
            after=after,
            far=tuple(i for i in range(len(operands) + 2) if i != 2 or not operands),
            scratch=scratch,
        )
        for (chunk, part), array in zip(pieces, made[len(outs) :]):
            weights[chunk][part] = array
        return made

    scratch = [
        pltpu.VMEM(context.shape, context.dtype),
        pltpu.VMEM(out_grad.shape, out_grad.dtype),
        dma((PIECES * len(LOADS[0]),)),
        dma((2,)),
    ]
    partial_shape = [shape(kept_rows.shape[0], kept_rows.shape[1], 128)]
    partial = load(
        0, masked_kernel, "masked", (context, out_grad, kept_rows), partial_shape, scratch, (packed[0],)
    )[0]
    route = call(
        route_kernel, "route", (ids, probs), [shape(3, token_count, 384)], after=(partial,)
    )[0]
    own, other = call(
        split_kernel, "split", tuple(arrived), [shape(ROWS, columns)] * 2, after=(route,)
    )
    own_far = swap(own, "tensor", 1)
    crossed = swap(other, "tensor", 2)

    def load_more(which, after):
        scratch = [dma((PIECES * len(LOADS[which]),))]
        kernel = functools.partial(load_kernel, LOADS[which])
        return load(which, kernel, "load", (), [], scratch, (after,))[0]

    def hold(value, after, cost=0):
        return call(pass_kernel, "hold", (value,), [value], after=(after,), aliases={0: 0}, cost=cost)[0]

    crossed = hold(crossed, load_more(1, own))
    crossed_far = swap(crossed, "tensor", 1)
    last = load_more(2, crossed)
    pieces = (own, own_far, crossed, crossed_far)

    hidden, remote = [], []
    for k, width in enumerate(CHUNKS):
        made = call(
            hidden_kernel,
            "hidden",
            (*pieces, *weights[k]),
            [shape(ROWS, width), shape(REMOTE, width)],
            after=(last,),
            scratch=[pltpu.VMEM((ROWS, depth), jnp.bfloat16)],
            cost=20 if k == 0 else 0,
        )
        hidden.append(made[0])
        remote.append(made[1])
        last = made[0]
    across = [swap(part, "tensor", 2) for part in remote]
    own_rows = call(merge_kernel, "merge", tuple(hidden), [shape(MOST, HALF)])[0]
    own_across = swap(own_rows, "tensor", 2)
    hidden_far = [swap(part, "tensor", 1) for part in hidden]

    def add(pieces, parts, total, after):
        rows = parts[0].shape[0]
        operands = (*parts, down_weight) + (() if total is None else (total,))
        return call(
            functools.partial(down_add_kernel, pieces, total is not None),
            "down_add",
            operands,
            [shape(rows, columns, dtype=f32)],
            after=after,
        )[0]

    total, step = None, own_rows
    held = hold(partial, own_rows)
    for k, start in enumerate(STARTS):
        if k == 2:
            pair = call(
                sum_kernel, "pair_sum", (held, swap(held, "rank", 1)), [partial], after=(total,)
            )[0]
            step = pair
        if k == 3:
            operands = [part for near_far in zip(hidden, hidden_far) for part in near_far]
            finished = call(
                down_own_kernel,
                "down_own",
                (*operands, down_weight),
                [shape(MOST, columns)] * OWNERS,
                after=(total,),
            )
            returned, own_result = finished[:3], finished[3]
            masked_grad = call(
                sum_kernel,
                "masked_sum",
                (pair, swap(pair, "rank", 2)),
                [shape(*partial.shape, dtype=f32)],
                after=(own_result,),
            )[0]
            step = masked_grad
        near = hold(across[k], step, 3)
        far = swap(near, "tensor", 1)
        total = add(((start, 0),), (near,), total, ())
        total = add(((start, 1),), (far,), total, ())
        step = total
    backs = call(
        back_kernel, "back", (total, *returned), [shape(2 * MOST, columns)] * 3
    )
    lists = [swap(backs[s - 1], "rank", s) for s in (1, 2, 3)]
    near = hold(own_across, backs[0], 3)
    far = swap(near, "tensor", 1)
    mine = add(((0, 0),), (near,), None, ())
    lists[0] = hold(lists[0], lists[1], 4)
    mine = add(((0, 1),), (far,), mine, (lists[0],))
    layer_output, router = call(
        combine_kernel,
        "combine",
        (own_result, mine, *lists, route, out_grad),
        [shape(token_count, columns), shape(8, token_count, dtype=f32)],
    )
    routers = [router] + [swap(router, "tensor", t) for t in (1, 2, 3)]
    router_grad = call(router_kernel, "router", tuple(routers), [shape(2, token_count, dtype=f32)])[0]
    return (layer_output, router_grad.T, masked_grad)


def solution(mesh):
    ranks, tensors = mesh.shape["rank"], mesh.shape["tensor"]
    body = routed if (ranks, tensors) == (4, 4) else shards
    return jax.shard_map(
        body,
        mesh=mesh,
        in_specs=(
            P(("groups", "rank"), "tensor"),
            P(("groups", "rank"), "tensor"),
            P(("groups", "rank"), None),
            P(("groups", "rank"), None),
            P(("groups", "rank"), None),
            P(None, ("rank", "tensor")),
            P(None, ("rank", "tensor")),
            P("rank", "tensor"),
            P("tensor", None),
        ),
        out_specs=(
            P(("groups", "rank"), "tensor"),
            P(("groups", "rank"), None),
            P(("groups", "tensor"), None, None),
        ),
        check_vma=False,
    )
```

```python
import functools
import jax
import jax.numpy as jnp
from jax import lax
from jax.experimental import pallas as pl
from jax.experimental.pallas import tpu as pltpu
from jax.sharding import PartitionSpec as P

FF = 7168
MOST = 40


def route_tables(expert_ids, gate_probs, rank_count, rank_units, per_rank, capacity):
    token_count = expert_ids.shape[0]
    owners = jnp.arange(rank_count, dtype=jnp.int32)
    first_expert = owners * rank_units // FF
    served = first_expert[:, None] + jnp.arange(per_rank, dtype=jnp.int32)[None, :]
    matches = expert_ids[None, :, None, :] == served[:, None, :, None]
    zero_weight = jnp.zeros((), jnp.bfloat16)
    weights = jnp.sum(jnp.where(matches, gate_probs[None, :, None, :], zero_weight), axis=3)
    member = jnp.any(matches, axis=(2, 3))
    position = jnp.cumsum(member.astype(jnp.int32), axis=1) - 1
    slot_ids = jnp.arange(capacity, dtype=jnp.int32)
    picked = member[:, None, :] & (position[:, None, :] == slot_ids[None, :, None])
    token_index = jnp.arange(token_count, dtype=jnp.int32)
    row_index = jnp.sum(jnp.where(picked, token_index[None, None, :], 0), axis=2)
    filled = jnp.any(picked, axis=2)
    slot_weight = jnp.where(filled[:, :, None], weights[owners[:, None], row_index], zero_weight)
    return (matches, row_index, filled, slot_weight)


def shards(
    tokens,
    out_grad,
    context,
    expert_ids,
    gate_probs,
    gate_weight,
    up_weight,
    down_weight,
    kept_rows,
):
    rank_count = lax.axis_size("rank")
    tensor_count = lax.axis_size("tensor")
    dev_units = gate_weight.shape[1]
    rank_units = dev_units * tensor_count
    per_rank = max(1, rank_units // FF)
    unit_span = min(rank_units, FF)
    token_count = tokens.shape[0]
    column_count = tokens.shape[1]
    capacity = min(MOST * per_rank, token_count)
    zero_value = jnp.zeros((), jnp.bfloat16)
    matches, row_index, filled, slot_weight = route_tables(
        expert_ids, gate_probs, rank_count, rank_units, per_rank, capacity
    )
    grad_send = jnp.where(filled[:, :, None], out_grad[row_index], zero_value)
    whole_rows = lax.all_gather(tokens, "tensor", axis=1, tiled=True)
    token_send = jnp.where(filled[:, :, None], whole_rows[row_index], zero_value)
    flat_index = row_index.reshape(-1)
    owner_rows = jnp.arange(rank_count, dtype=jnp.int32)[:, None]
    received = (
        lax.all_to_all(token_send, "rank", split_axis=0, concat_axis=0, tiled=True),
        lax.all_to_all(grad_send, "rank", split_axis=0, concat_axis=0, tiled=True),
        lax.all_to_all(slot_weight, "rank", split_axis=0, concat_axis=0, tiled=True),
    )
    routed_rows = received[0]
    source_count = routed_rows.shape[0]
    item_count = routed_rows.shape[1]
    row_count = source_count * item_count
    token_rows = routed_rows.reshape(row_count, routed_rows.shape[2])
    gate_act = jnp.dot(token_rows, gate_weight, preferred_element_type=jnp.float32)
    up_act = jnp.dot(token_rows, up_weight, preferred_element_type=jnp.float32)
    hidden = (jax.nn.silu(gate_act) * up_act).astype(jnp.bfloat16)

    def add_units(totals, shard_piece):
        width = shard_piece.shape[1]
        if per_rank == 1:
            return (
                totals + jnp.dot(shard_piece, down_weight, preferred_element_type=jnp.float32)[None]
            )
        unit_index = jnp.arange(width, dtype=jnp.int32)
        products = []
        for which in range(per_rank):
            inside = (unit_index // unit_span == which)[None, :]
            masked_piece = jnp.where(inside, shard_piece, zero_value)
            products.append(jnp.dot(masked_piece, down_weight, preferred_element_type=jnp.float32))
        return totals + jnp.stack(products)

    zero_out = jnp.zeros((per_rank, row_count, down_weight.shape[1]), jnp.float32)
    expert_out = add_units(zero_out, lax.all_gather(hidden, "tensor", axis=1, tiled=True))
    grad_flat = received[1].reshape(row_count, column_count).astype(jnp.float32)
    weight_flat = received[2].reshape(row_count, per_rank).astype(jnp.float32)
    output_part = jnp.sum(expert_out * jnp.transpose(weight_flat)[:, :, None], axis=0)
    router_part = jnp.transpose(jnp.sum(expert_out * grad_flat[None], axis=2))
    router_part = lax.psum(router_part, "tensor")
    output_back = lax.all_to_all(
        output_part.reshape(source_count, item_count, column_count),
        "rank",
        split_axis=0,
        concat_axis=0,
        tiled=True,
    )
    router_back = lax.all_to_all(
        router_part.reshape(source_count, item_count, per_rank),
        "rank",
        split_axis=0,
        concat_axis=0,
        tiled=True,
    )
    output_rows = jnp.where(filled[:, :, None], output_back, 0.0).reshape(-1, column_count)
    layer_sum = jnp.zeros((token_count, column_count), jnp.float32).at[flat_index].add(output_rows)
    layer_output = layer_sum.astype(jnp.bfloat16)
    router_terms = jnp.where(filled[:, :, None], router_back, 0.0)
    per_token = (
        jnp.zeros((rank_count, token_count, per_rank), jnp.float32)
        .at[owner_rows, row_index]
        .add(router_terms)
    )
    router_grad = jnp.sum(jnp.where(matches, per_token[:, :, :, None], 0.0), axis=(0, 2))
    local_blocks = kept_rows.shape[0]
    keep_count = kept_rows.shape[1]
    picked_context = jnp.take(context, kept_rows.reshape(-1), axis=1).reshape(
        token_count, local_blocks, keep_count
    )
    grad_blocks = out_grad.reshape(token_count, local_blocks, 128)
    local_grad = jnp.einsum(
        "tck,tcj->ckj", picked_context, grad_blocks, preferred_element_type=jnp.float32
    )
    masked_grad = lax.psum(local_grad, "rank")
    return (layer_output, router_grad, masked_grad)


OWNERS = 4
LISTS = 8
ROWS = OWNERS * MOST
REMOTE = ROWS - MOST
CHUNKS = (1408, 1024, 1152)
STARTS = (0, 1408, 2432)
HALF = FF // 2
BLOCK = 256
FLUSH = ((), (1,), (0, 2))
OWN_NEAR = ((0, 0, 0), (HALF // 2, 0, 0))
OWN_FAR = ((0, 0, 1), (HALF // 2, 0, 1))
ANY = pl.BlockSpec(memory_space=pl.ANY)
HBM = pl.BlockSpec(memory_space=pltpu.HBM)
VMEM = pl.BlockSpec(memory_space=pltpu.VMEM)


def call(kernel, name, operands, outs, *, after=(), far=(), scratch=(), aliases=None, cost=0, limit=3):
    count, late = len(operands), len(after)
    operands = [
        pltpu.with_memory_space_constraint(x, pltpu.HBM) if i in far else x
        for i, x in enumerate(operands)
    ]

    def body(*refs):
        place = (lax.axis_index("rank"), lax.axis_index("tensor"))
        kernel(place, *refs[:count], *refs[count + late :])

    return pl.pallas_call(
        body,
        out_shape=outs,
        in_specs=[HBM if i in far else VMEM for i in range(count)] + [ANY] * late,
        out_specs=[VMEM] * len(outs),
        scratch_shapes=scratch,
        name=name,
        input_output_aliases=aliases or {},
        compiler_params=pltpu.CompilerParams(vmem_limit_bytes=limit * 2**20),
        cost_estimate=pl.CostEstimate(flops=0, bytes_accessed=int(cost * 3e6), transcendentals=0),
    )(*operands, *after)


def shape(*dims, dtype=jnp.bfloat16):
    return jax.ShapeDtypeStruct(dims, dtype)


def product(left, right):
    return jnp.dot(left, right, preferred_element_type=jnp.float32)


def slot_codes(place, ids_ref):
    rank, chip = place[0], place[1] // 2
    count = ids_ref.shape[1]
    lists = lax.broadcasted_iota(jnp.int32, (LISTS, count), 0)
    experts = 2 * (rank ^ (lists // 2)) + (chip ^ (lists % 2))
    chosen = [ids_ref[k : k + 1, :] == experts for k in range(2)]
    member = jnp.where(chosen[0] | chosen[1], 1.0, 0.0).astype(jnp.bfloat16)
    earlier = lax.broadcasted_iota(jnp.int32, (count, count), 0) < lax.broadcasted_iota(
        jnp.int32, (count, count), 1
    )
    before = jnp.where(earlier, 1.0, 0.0).astype(jnp.bfloat16)
    position = product(member, before)
    return [jnp.where(c, position, -1.0) for c in chosen]


def slot_matrix(code, value=1.0):
    count = code.shape[1]
    slots = lax.broadcasted_iota(jnp.int32, (MOST, count), 0).astype(jnp.float32)
    return jnp.concatenate(
        [jnp.where(code[q : q + 1] == slots, value, 0.0) for q in range(LISTS)], axis=0
    )


def pack_kernel(place, ids_ref, tokens_ref, *refs):
    outs, (ids, tokens, sems) = refs[:OWNERS], refs[OWNERS:]
    copies = [
        pltpu.make_async_copy(ids_ref, ids, sems.at[0]),
        pltpu.make_async_copy(tokens_ref, tokens, sems.at[1]),
    ]
    for copy in copies:
        copy.start()
    copies[0].wait()
    first, second = slot_codes(place, ids)
    pick = slot_matrix(jnp.maximum(first, second)).astype(jnp.bfloat16)
    copies[1].wait()
    rows = product(pick, tokens[...])
    for s in range(OWNERS):
        outs[s][...] = rows[2 * MOST * s : 2 * MOST * (s + 1)].astype(jnp.bfloat16)


def route_kernel(place, ids_ref, probs_ref, out_ref):
    count = ids_ref.shape[1]
    codes = slot_codes(place, ids_ref)
    probs = [probs_ref[k : k + 1, :].astype(jnp.float32) for k in range(2)]
    weighted = slot_matrix(codes[0], probs[0]) + slot_matrix(codes[1], probs[1])
    for k, pick in enumerate((slot_matrix(codes[0]), slot_matrix(codes[1]), weighted)):
        padded = jnp.concatenate([pick, jnp.zeros((64, count), jnp.float32)], axis=0)
        out_ref[k] = jnp.transpose(padded).astype(jnp.bfloat16)


def split_kernel(place, *refs):
    own_ref, other_ref = refs[OWNERS:]
    order = [refs[s][...].astype(jnp.float32) for s in (1, 2, 3, 0)]
    own_ref[...] = jnp.concatenate([d[:MOST] for d in order], axis=0).astype(jnp.bfloat16)
    other_ref[...] = jnp.concatenate([d[MOST:] for d in order], axis=0).astype(jnp.bfloat16)


def masked_kernel(place, context_hbm, grad_hbm, kept_hbm, gate_hbm, up_hbm, out_ref, *scratch):
    context, grad, kept_ref, sems = scratch
    pairs = ((context_hbm, context), (grad_hbm, grad), (kept_hbm, kept_ref))
    copies = [pltpu.make_async_copy(*pair, sems.at[i]) for i, pair in enumerate(pairs)]
    for copy in copies:
        copy.start()
    features, keep = context.shape[1], kept_ref.shape[1]
    index = lax.broadcasted_iota(jnp.int32, (features, keep), 0)
    for copy in copies:
        copy.wait()
    for c in range(kept_ref.shape[0]):
        pick = jnp.where(index == kept_ref[c : c + 1, :], 1.0, 0.0).astype(jnp.bfloat16)
        picked = product(context[...], pick).astype(jnp.bfloat16)
        part = lax.dot_general(
            picked,
            grad[:, 128 * c : 128 * (c + 1)],
            (((0,), (0,)), ((), ())),
            preferred_element_type=jnp.float32,
        )
        out_ref[c] = part


def pass_kernel(place, in_ref, out_ref):
    pass


def sum_kernel(place, left, right, out_ref):
    total = left[...].astype(jnp.float32) + right[...].astype(jnp.float32)
    out_ref[...] = total.astype(out_ref.dtype)


def masked_sum_kernel(place, left, right, out_ref, token_ref):
    sum_kernel(place, left, right, out_ref)
    token_ref[...] = jnp.zeros_like(token_ref)


def hidden_kernel(first, place, a0, a1, a2, a3, gate_ref, up_ref, out_ref, remote_ref, rows):
    for j, piece in enumerate((a0, a1, a2, a3)):
        width = piece.shape[1]
        start = pl.multiple_of((place[1] ^ j) * width, width)
        rows[:, pl.ds(start, width)] = piece[...]
    for start in range(0, out_ref.shape[1], BLOCK):
        columns = slice(start, min(start + BLOCK, out_ref.shape[1]))
        units = slice(first + columns.start, first + columns.stop)
        gate = product(rows[...], gate_ref[:, units])
        up = product(rows[...], up_ref[:, units])
        hidden = gate / (1.0 + jnp.exp(-gate)) * up
        out_ref[:, columns] = hidden.astype(jnp.bfloat16)
        remote_ref[:, columns] = hidden[:REMOTE].astype(jnp.bfloat16)


def merge_kernel(place, *refs):
    parts, (first_ref, second_ref, own_ref) = refs[: len(CHUNKS)], refs[len(CHUNKS) :]
    for start, width, part in zip(STARTS, CHUNKS, parts):
        own = part[...].astype(jnp.float32)[REMOTE:]
        own_ref[:, start : start + width] = own.astype(jnp.bfloat16)
        for half_ref, begin in ((first_ref, 0), (second_ref, HALF // 2)):
            low, high = max(start, begin), min(start + width, begin + HALF // 2)
            if low < high:
                half_ref[:, low - begin : high - begin] = part[:, low - start : high - start]


def down_part(place, part, down_ref, start, flip, core):
    chip, own = (place[1] // 2) ^ flip, (place[1] % 2) ^ core
    rows = pl.ds(pl.multiple_of((2 * chip + own) * HALF + start, 128), part.shape[1])
    return product(part[...], down_ref[rows, :])


def down_add_kernel(pieces, has_total, place, *refs):
    parts, down_ref, refs = refs[: len(pieces)], refs[len(pieces)], refs[len(pieces) + 1 :]
    total = refs[0][...] if has_total else None
    for (start, flip, core), part in zip(pieces, parts):
        term = down_part(place, part, down_ref, start, flip, core)
        total = term if total is None else total + term
    refs[-1][...] = total


def back_kernel(place, total_ref, mine_ref, *outs):
    for s in range(OWNERS - 1):
        both = [ref[MOST * s : MOST * (s + 1), :] for ref in (mine_ref, total_ref)]
        outs[s][...] = jnp.concatenate(both, axis=0).astype(jnp.bfloat16)
    outs[-1][...] = mine_ref[REMOTE:, :].astype(jnp.bfloat16)


def combine_kernel(place, own, other, b1, b2, b3, route_ref, grad_ref, layer_ref, router_ref):
    count, columns = grad_ref.shape
    stacked = [ref[...].astype(jnp.float32) for ref in (own, other, b1, b2, b3)]
    stacked.append(jnp.zeros((64, columns), jnp.float32))
    rows = jnp.concatenate(stacked, axis=0).astype(jnp.bfloat16)
    grad = grad_ref[...].astype(jnp.float32)
    layer_ref[...] = product(route_ref[2], rows).astype(jnp.bfloat16)
    lane = lax.broadcasted_iota(jnp.int32, (count, 128), 1)
    scores = jnp.zeros((count, 128), jnp.float32)
    for k in range(2):
        score = jnp.sum(grad * product(route_ref[k], rows), axis=1, keepdims=True)
        scores = jnp.where(lane == k, score, scores)
    router_ref[...] = jnp.transpose(scores)[:8]


def router_kernel(place, p0, p1, p2, p3, out_ref):
    out_ref[...] = ((p0[...] + p1[...]) + (p2[...] + p3[...]))[:2]


def swap(value, axis, by):
    return lax.ppermute(value, axis, [(i, i ^ by) for i in range(4)])


def routed(
    tokens,
    out_grad,
    context,
    expert_ids,
    gate_probs,
    gate_weight,
    up_weight,
    down_weight,
    kept_rows,
):
    token_count, columns = tokens.shape
    depth = gate_weight.shape[0]
    f32 = jnp.float32
    dma = pltpu.SemaphoreType.DMA
    ids, probs = expert_ids.T, gate_probs.T

    packed = call(
        pack_kernel,
        "pack",
        (ids, tokens),
        [shape(2 * MOST, columns)] * OWNERS,
        far=(0, 1),
        scratch=[pltpu.VMEM(ids.shape, ids.dtype), pltpu.VMEM(tokens.shape, tokens.dtype), dma((2,))],
    )
    arrived = [packed[0]] + [swap(packed[s], "rank", s) for s in (1, 2, 3)]
    blocks = (kept_rows.shape[0], kept_rows.shape[1], 128)
    partial = call(
        masked_kernel,
        "masked",
        (context, out_grad, kept_rows, gate_weight, up_weight),
        [shape(*blocks, dtype=f32)],
        after=(packed[0],),
        far=(0, 1, 2, 3, 4),
        limit=4,
        scratch=[
            pltpu.VMEM(context.shape, context.dtype),
            pltpu.VMEM(out_grad.shape, out_grad.dtype),
            pltpu.VMEM(kept_rows.shape, kept_rows.dtype),
            dma((3,)),
        ],
    )[0]
    route = call(
        route_kernel, "route", (ids, probs), [shape(3, token_count, 384)], after=(partial,)
    )[0]
    own, other = call(
        split_kernel, "split", tuple(arrived), [shape(ROWS, columns)] * 2, after=(route,)
    )
    own_far = swap(own, "tensor", 1)
    crossed = swap(other, "tensor", 2)

    def hold(value, *after):
        return call(pass_kernel, "hold", (value,), [value], after=after, aliases={0: 0})[0]

    held = hold(partial, own)
    crossed = hold(crossed, own)
    crossed_far = swap(crossed, "tensor", 1)
    pieces = (own, own_far, crossed, crossed_far)

    hidden, remote, last = [], [], route
    for k, width in enumerate(CHUNKS):
        made = call(
            functools.partial(hidden_kernel, STARTS[k]),
            "hidden",
            (*pieces, gate_weight, up_weight),
            [shape(ROWS, width), shape(REMOTE, width)],
            after=(last,),
            scratch=[pltpu.VMEM((ROWS, depth), jnp.bfloat16)],
            cost=20 if k == 0 else 0,
        )
        hidden.append(made[0])
        remote.append(made[1])
        last = made[0]
        if k == 0:
            last = pair = call(
                sum_kernel, "pair_sum", (held, swap(held, "rank", 1)), [shape(*blocks)], after=(last,)
            )[0]
    across = [swap(part, "tensor", 2) for part in remote]
    *full, own_rows = call(
        merge_kernel,
        "merge",
        tuple(hidden),
        [shape(ROWS, HALF // 2)] * 2 + [shape(MOST, HALF)],
    )
    full_far = [swap(part, "tensor", 1) for part in full]
    own_across = swap(own_rows, "tensor", 2)

    def add(pieces, parts, total, after=()):
        rows = parts[0].shape[0]
        operands = (*parts, down_weight) + (() if total is None else (total,))
        return call(
            functools.partial(down_add_kernel, pieces, total is not None),
            "down_add",
            operands,
            [shape(rows, columns, dtype=f32)],
            after=after,
        )[0]

    total, step = None, own_rows
    fars = []
    for k, start in enumerate(STARTS):
        if k == 1:
            masked_grad, step = call(
                masked_sum_kernel,
                "masked_sum",
                (pair, swap(pair, "rank", 2)),
                [shape(*blocks, dtype=f32), shape(8, 128, dtype=f32)],
                after=(total,),
            )
        if k == 2:
            mine = call(
                functools.partial(down_add_kernel, OWN_NEAR, False),
                "down_add",
                (*full, down_weight),
                [shape(ROWS, columns, dtype=f32)],
                after=(total,),
            )[0]
            step = mine
        near = hold(across[k], step)
        far = swap(near, "tensor", 1)
        total = add(((start, 1, 0),), (near,), total)
        fars.append(((start, 1, 1), far))
        for j in FLUSH[k]:
            total = add((fars[j][0],), (fars[j][1],), total)
        step = total
    mine = add(OWN_FAR, full_far, mine, (total,))
    *backs, own = call(
        back_kernel,
        "back",
        (total, mine),
        [shape(2 * MOST, columns)] * 3 + [shape(MOST, columns)],
    )
    lists = [swap(backs[s - 1], "rank", s) for s in (1, 2, 3)]
    near = hold(own_across, *lists)
    far = swap(near, "tensor", 1)
    last = add(((0, 1, 0),), (near,), None)
    last = add(((0, 1, 1),), (far,), last)
    layer_output, router = call(
        combine_kernel,
        "combine",
        (own, last, *lists, route, out_grad),
        [shape(token_count, columns), shape(8, token_count, dtype=f32)],
    )
    routers = [router] + [swap(router, "tensor", t) for t in (1, 2, 3)]
    router_grad = call(router_kernel, "router", tuple(routers), [shape(2, token_count, dtype=f32)])[0]
    return (layer_output, router_grad.T, masked_grad)


def solution(mesh):
    ranks, tensors = mesh.shape["rank"], mesh.shape["tensor"]
    body = routed if (ranks, tensors) == (4, 4) else shards
    return jax.shard_map(
        body,
        mesh=mesh,
        in_specs=(
            P(("groups", "rank"), "tensor"),
            P(("groups", "rank"), "tensor"),
            P(("groups", "rank"), None),
            P(("groups", "rank"), None),
            P(("groups", "rank"), None),
            P(None, ("rank", "tensor")),
            P(None, ("rank", "tensor")),
            P("rank", "tensor"),
            P("tensor", None),
        ),
        out_specs=(
            P(("groups", "rank"), "tensor"),
            P(("groups", "rank"), None),
            P(("groups", "tensor"), None, None),
        ),
        check_vma=False,
    )
```

```python
import functools
import jax
import jax.numpy as jnp
from jax import lax
from jax.experimental import pallas as pl
from jax.experimental.pallas import tpu as pltpu
from jax.sharding import PartitionSpec as P

FF = 7168
MOST = 40


def route_tables(expert_ids, gate_probs, rank_count, rank_units, per_rank, capacity):
    token_count = expert_ids.shape[0]
    owners = jnp.arange(rank_count, dtype=jnp.int32)
    first_expert = owners * rank_units // FF
    served = first_expert[:, None] + jnp.arange(per_rank, dtype=jnp.int32)[None, :]
    matches = expert_ids[None, :, None, :] == served[:, None, :, None]
    zero_weight = jnp.zeros((), jnp.bfloat16)
    weights = jnp.sum(jnp.where(matches, gate_probs[None, :, None, :], zero_weight), axis=3)
    member = jnp.any(matches, axis=(2, 3))
    position = jnp.cumsum(member.astype(jnp.int32), axis=1) - 1
    slot_ids = jnp.arange(capacity, dtype=jnp.int32)
    picked = member[:, None, :] & (position[:, None, :] == slot_ids[None, :, None])
    token_index = jnp.arange(token_count, dtype=jnp.int32)
    row_index = jnp.sum(jnp.where(picked, token_index[None, None, :], 0), axis=2)
    filled = jnp.any(picked, axis=2)
    slot_weight = jnp.where(filled[:, :, None], weights[owners[:, None], row_index], zero_weight)
    return (matches, row_index, filled, slot_weight)


def shards(
    tokens,
    out_grad,
    context,
    expert_ids,
    gate_probs,
    gate_weight,
    up_weight,
    down_weight,
    kept_rows,
):
    rank_count = lax.axis_size("rank")
    tensor_count = lax.axis_size("tensor")
    dev_units = gate_weight.shape[1]
    rank_units = dev_units * tensor_count
    per_rank = max(1, rank_units // FF)
    unit_span = min(rank_units, FF)
    token_count = tokens.shape[0]
    column_count = tokens.shape[1]
    capacity = min(MOST * per_rank, token_count)
    zero_value = jnp.zeros((), jnp.bfloat16)
    matches, row_index, filled, slot_weight = route_tables(
        expert_ids, gate_probs, rank_count, rank_units, per_rank, capacity
    )
    grad_send = jnp.where(filled[:, :, None], out_grad[row_index], zero_value)
    whole_rows = lax.all_gather(tokens, "tensor", axis=1, tiled=True)
    token_send = jnp.where(filled[:, :, None], whole_rows[row_index], zero_value)
    flat_index = row_index.reshape(-1)
    owner_rows = jnp.arange(rank_count, dtype=jnp.int32)[:, None]
    received = (
        lax.all_to_all(token_send, "rank", split_axis=0, concat_axis=0, tiled=True),
        lax.all_to_all(grad_send, "rank", split_axis=0, concat_axis=0, tiled=True),
        lax.all_to_all(slot_weight, "rank", split_axis=0, concat_axis=0, tiled=True),
    )
    routed_rows = received[0]
    source_count = routed_rows.shape[0]
    item_count = routed_rows.shape[1]
    row_count = source_count * item_count
    token_rows = routed_rows.reshape(row_count, routed_rows.shape[2])
    gate_act = jnp.dot(token_rows, gate_weight, preferred_element_type=jnp.float32)
    up_act = jnp.dot(token_rows, up_weight, preferred_element_type=jnp.float32)
    hidden = (jax.nn.silu(gate_act) * up_act).astype(jnp.bfloat16)

    def add_units(totals, shard_piece):
        width = shard_piece.shape[1]
        if per_rank == 1:
            return (
                totals + jnp.dot(shard_piece, down_weight, preferred_element_type=jnp.float32)[None]
            )
        unit_index = jnp.arange(width, dtype=jnp.int32)
        products = []
        for which in range(per_rank):
            inside = (unit_index // unit_span == which)[None, :]
            masked_piece = jnp.where(inside, shard_piece, zero_value)
            products.append(jnp.dot(masked_piece, down_weight, preferred_element_type=jnp.float32))
        return totals + jnp.stack(products)

    zero_out = jnp.zeros((per_rank, row_count, down_weight.shape[1]), jnp.float32)
    expert_out = add_units(zero_out, lax.all_gather(hidden, "tensor", axis=1, tiled=True))
    grad_flat = received[1].reshape(row_count, column_count).astype(jnp.float32)
    weight_flat = received[2].reshape(row_count, per_rank).astype(jnp.float32)
    output_part = jnp.sum(expert_out * jnp.transpose(weight_flat)[:, :, None], axis=0)
    router_part = jnp.transpose(jnp.sum(expert_out * grad_flat[None], axis=2))
    router_part = lax.psum(router_part, "tensor")
    output_back = lax.all_to_all(
        output_part.reshape(source_count, item_count, column_count),
        "rank",
        split_axis=0,
        concat_axis=0,
        tiled=True,
    )
    router_back = lax.all_to_all(
        router_part.reshape(source_count, item_count, per_rank),
        "rank",
        split_axis=0,
        concat_axis=0,
        tiled=True,
    )
    output_rows = jnp.where(filled[:, :, None], output_back, 0.0).reshape(-1, column_count)
    layer_sum = jnp.zeros((token_count, column_count), jnp.float32).at[flat_index].add(output_rows)
    layer_output = layer_sum.astype(jnp.bfloat16)
    router_terms = jnp.where(filled[:, :, None], router_back, 0.0)
    per_token = (
        jnp.zeros((rank_count, token_count, per_rank), jnp.float32)
        .at[owner_rows, row_index]
        .add(router_terms)
    )
    router_grad = jnp.sum(jnp.where(matches, per_token[:, :, :, None], 0.0), axis=(0, 2))
    local_blocks = kept_rows.shape[0]
    keep_count = kept_rows.shape[1]
    picked_context = jnp.take(context, kept_rows.reshape(-1), axis=1).reshape(
        token_count, local_blocks, keep_count
    )
    grad_blocks = out_grad.reshape(token_count, local_blocks, 128)
    local_grad = jnp.einsum(
        "tck,tcj->ckj", picked_context, grad_blocks, preferred_element_type=jnp.float32
    )
    masked_grad = lax.psum(local_grad, "rank")
    return (layer_output, router_grad, masked_grad)


OWNERS = 4
LISTS = 8
ROWS = OWNERS * MOST
REMOTE = ROWS - MOST
CHUNKS = (1152, 1024, 1408)
STARTS = (0, 1152, 2176)
HALF = FF // 2
BLOCK = 256
SEND_ORDER = (2, 3, 1)
FLUSH = ((), (0, 1), (2,))
OWN_NEAR = ((0, 0, 0), (HALF // 2, 0, 0))
OWN_FAR = ((0, 0, 1), (HALF // 2, 0, 1))
ANY = pl.BlockSpec(memory_space=pl.ANY)
HBM = pl.BlockSpec(memory_space=pltpu.HBM)
VMEM = pl.BlockSpec(memory_space=pltpu.VMEM)


def call(kernel, name, operands, outs, *, after=(), far=(), scratch=(), aliases=None, cost=0, limit=3):
    count, late = len(operands), len(after)
    operands = [
        pltpu.with_memory_space_constraint(x, pltpu.HBM) if i in far else x
        for i, x in enumerate(operands)
    ]

    def body(*refs):
        place = (lax.axis_index("rank"), lax.axis_index("tensor"))
        kernel(place, *refs[:count], *refs[count + late :])

    return pl.pallas_call(
        body,
        out_shape=outs,
        in_specs=[HBM if i in far else VMEM for i in range(count)] + [ANY] * late,
        out_specs=[VMEM] * len(outs),
        scratch_shapes=scratch,
        name=name,
        input_output_aliases=aliases or {},
        compiler_params=pltpu.CompilerParams(vmem_limit_bytes=limit * 2**20),
        cost_estimate=pl.CostEstimate(flops=0, bytes_accessed=int(cost * 3e6), transcendentals=0),
    )(*operands, *after)


def shape(*dims, dtype=jnp.bfloat16):
    return jax.ShapeDtypeStruct(dims, dtype)


def product(left, right):
    return jnp.dot(left, right, preferred_element_type=jnp.float32)


def slot_codes(place, ids_ref):
    rank, chip = place[0], place[1] // 2
    count = ids_ref.shape[1]
    lists = lax.broadcasted_iota(jnp.int32, (LISTS, count), 0)
    experts = 2 * (rank ^ (lists // 2)) + (chip ^ (lists % 2))
    chosen = [ids_ref[k : k + 1, :] == experts for k in range(2)]
    member = jnp.where(chosen[0] | chosen[1], 1.0, 0.0).astype(jnp.bfloat16)
    earlier = lax.broadcasted_iota(jnp.int32, (count, count), 0) < lax.broadcasted_iota(
        jnp.int32, (count, count), 1
    )
    before = jnp.where(earlier, 1.0, 0.0).astype(jnp.bfloat16)
    position = product(member, before)
    return [jnp.where(c, position, -1.0) for c in chosen]


def slot_matrix(code, value=1.0):
    count = code.shape[1]
    slots = lax.broadcasted_iota(jnp.int32, (MOST, count), 0).astype(jnp.float32)
    return jnp.concatenate(
        [jnp.where(code[q : q + 1] == slots, value, 0.0) for q in range(LISTS)], axis=0
    )


def pack_kernel(place, ids_ref, tokens_ref, gate_hbm, up_hbm, *refs):
    outs, (ids, tokens, sems) = refs[:OWNERS], refs[OWNERS:]
    copies = [
        pltpu.make_async_copy(ids_ref, ids, sems.at[0]),
        pltpu.make_async_copy(tokens_ref, tokens, sems.at[1]),
    ]
    for copy in copies:
        copy.start()
    copies[0].wait()
    first, second = slot_codes(place, ids)
    pick = slot_matrix(jnp.maximum(first, second)).astype(jnp.bfloat16)
    copies[1].wait()
    rows = product(pick, tokens[...])
    for s in range(OWNERS):
        outs[s][...] = rows[2 * MOST * s : 2 * MOST * (s + 1)].astype(jnp.bfloat16)


def route_kernel(place, ids_ref, probs_ref, out_ref):
    count = ids_ref.shape[1]
    codes = slot_codes(place, ids_ref)
    probs = [probs_ref[k : k + 1, :].astype(jnp.float32) for k in range(2)]
    weighted = slot_matrix(codes[0], probs[0]) + slot_matrix(codes[1], probs[1])
    for k, pick in enumerate((slot_matrix(codes[0]), slot_matrix(codes[1]), weighted)):
        padded = jnp.concatenate([pick, jnp.zeros((64, count), jnp.float32)], axis=0)
        out_ref[k] = jnp.transpose(padded).astype(jnp.bfloat16)


def split_kernel(place, *refs):
    own_ref, other_ref = refs[OWNERS:]
    order = [ref[...].astype(jnp.float32) for ref in (*reversed(refs[: OWNERS - 1]), refs[OWNERS - 1])]
    own_ref[...] = jnp.concatenate([d[:MOST] for d in order], axis=0).astype(jnp.bfloat16)
    other_ref[...] = jnp.concatenate([d[MOST:] for d in order], axis=0).astype(jnp.bfloat16)


def masked_kernel(place, context_hbm, grad_hbm, kept_hbm, out_ref, *scratch):
    context, grad, kept_ref, sems = scratch
    pairs = ((context_hbm, context), (grad_hbm, grad), (kept_hbm, kept_ref))
    copies = [pltpu.make_async_copy(*pair, sems.at[i]) for i, pair in enumerate(pairs)]
    for copy in copies:
        copy.start()
    features, keep = context.shape[1], kept_ref.shape[1]
    index = lax.broadcasted_iota(jnp.int32, (features, keep), 0)
    for copy in copies:
        copy.wait()
    for c in range(kept_ref.shape[0]):
        pick = jnp.where(index == kept_ref[c : c + 1, :], 1.0, 0.0).astype(jnp.bfloat16)
        picked = product(context[...], pick).astype(jnp.bfloat16)
        part = lax.dot_general(
            picked,
            grad[:, 128 * c : 128 * (c + 1)],
            (((0,), (0,)), ((), ())),
            preferred_element_type=jnp.float32,
        )
        out_ref[c] = part


def pass_kernel(place, in_ref, out_ref):
    pass


def sum_kernel(place, left, right, out_ref):
    total = left[...].astype(jnp.float32) + right[...].astype(jnp.float32)
    out_ref[...] = total.astype(out_ref.dtype)


def masked_sum_kernel(place, left, right, out_ref, token_ref):
    sum_kernel(place, left, right, out_ref)
    token_ref[...] = jnp.zeros_like(token_ref)


def features_of(place, by, width):
    return pl.ds(pl.multiple_of((place[1] ^ by) * width, width), width)


def begun_kernel(place, own, gate_ref, up_ref, gate_out, up_out):
    features = features_of(place, 0, own.shape[1])
    for start in range(0, gate_out.shape[1], BLOCK):
        units = slice(start, min(start + BLOCK, gate_out.shape[1]))
        gate_out[:, units] = product(own[...], gate_ref[features, units])
        up_out[:, units] = product(own[...], up_ref[features, units])


def hidden_kernel(first, place, a0, a1, a2, a3, *refs):
    begun, (gate_ref, up_ref, out_ref, remote_ref) = refs[:-4], refs[-4:]
    pieces = [(by, piece[...]) for by, piece in enumerate((a0, a1, a2, a3)) if by or not begun]
    for start in range(0, out_ref.shape[1], BLOCK):
        columns = slice(start, min(start + BLOCK, out_ref.shape[1]))
        units = slice(first + columns.start, first + columns.stop)
        acts = []
        for i, weight_ref in enumerate((gate_ref, up_ref)):
            act = begun[i][:, columns] if begun else None
            for by, piece in pieces:
                term = product(piece, weight_ref[features_of(place, by, piece.shape[1]), units])
                act = term if act is None else act + term
            acts.append(act)
        gate, up = acts
        hidden = gate / (1.0 + jnp.exp(-gate)) * up
        out_ref[:, columns] = hidden.astype(jnp.bfloat16)
        remote_ref[:, columns] = hidden[:REMOTE].astype(jnp.bfloat16)


def merge_kernel(place, *refs):
    parts, (first_ref, second_ref, own_ref) = refs[: len(CHUNKS)], refs[len(CHUNKS) :]
    for start, width, part in zip(STARTS, CHUNKS, parts):
        own = part[...].astype(jnp.float32)[REMOTE:]
        own_ref[:, start : start + width] = own.astype(jnp.bfloat16)
        for half_ref, begin in ((first_ref, 0), (second_ref, HALF // 2)):
            low, high = max(start, begin), min(start + width, begin + HALF // 2)
            if low < high:
                half_ref[:, low - begin : high - begin] = part[:, low - start : high - start]


def down_part(place, part, down_ref, start, flip, core):
    chip, own = (place[1] // 2) ^ flip, (place[1] % 2) ^ core
    rows = pl.ds(pl.multiple_of((2 * chip + own) * HALF + start, 128), part.shape[1])
    return product(part[...], down_ref[rows, :])


def down_add_kernel(pieces, has_total, place, *refs):
    parts, down_ref, refs = refs[: len(pieces)], refs[len(pieces)], refs[len(pieces) + 1 :]
    total = refs[0][...] if has_total else None
    for (start, flip, core), part in zip(pieces, parts):
        term = down_part(place, part, down_ref, start, flip, core)
        total = term if total is None else total + term
    refs[-1][...] = total


def back_kernel(place, total_ref, mine_ref, *outs):
    for s in range(OWNERS - 1):
        both = [ref[MOST * s : MOST * (s + 1), :] for ref in (mine_ref, total_ref)]
        outs[s][...] = jnp.concatenate(both, axis=0).astype(jnp.bfloat16)
    outs[-1][...] = mine_ref[REMOTE:, :].astype(jnp.bfloat16)


def combine_kernel(place, own, other, b3, b2, b1, route_ref, grad_ref, layer_ref, router_ref):
    count, columns = grad_ref.shape
    stacked = [ref[...].astype(jnp.float32) for ref in (own, other, b1, b2, b3)]
    stacked.append(jnp.zeros((64, columns), jnp.float32))
    rows = jnp.concatenate(stacked, axis=0).astype(jnp.bfloat16)
    grad = grad_ref[...].astype(jnp.float32)
    layer_ref[...] = product(route_ref[2], rows).astype(jnp.bfloat16)
    lane = lax.broadcasted_iota(jnp.int32, (count, 128), 1)
    scores = jnp.zeros((count, 128), jnp.float32)
    for k in range(2):
        score = jnp.sum(grad * product(route_ref[k], rows), axis=1, keepdims=True)
        scores = jnp.where(lane == k, score, scores)
    router_ref[...] = jnp.transpose(scores)[:8]


def router_kernel(place, p0, p1, p2, p3, out_ref):
    out_ref[...] = ((p0[...] + p1[...]) + (p2[...] + p3[...]))[:2]


def swap(value, axis, by):
    return lax.ppermute(value, axis, [(i, i ^ by) for i in range(4)])


def routed(
    tokens,
    out_grad,
    context,
    expert_ids,
    gate_probs,
    gate_weight,
    up_weight,
    down_weight,
    kept_rows,
):
    token_count, columns = tokens.shape
    depth = gate_weight.shape[0]
    f32 = jnp.float32
    dma = pltpu.SemaphoreType.DMA
    ids, probs = expert_ids.T, gate_probs.T

    packed = call(
        pack_kernel,
        "pack",
        (ids, tokens, gate_weight, up_weight),
        [shape(2 * MOST, columns)] * OWNERS,
        far=(0, 1, 2, 3),
        scratch=[pltpu.VMEM(ids.shape, ids.dtype), pltpu.VMEM(tokens.shape, tokens.dtype), dma((2,))],
    )
    sent = {s: swap(packed[s], "rank", s) for s in SEND_ORDER}
    arrived = [sent[3], sent[2], sent[1], packed[0]]
    blocks = (kept_rows.shape[0], kept_rows.shape[1], 128)
    partial = call(
        masked_kernel,
        "masked",
        (context, out_grad, kept_rows),
        [shape(*blocks, dtype=f32)],
        after=(packed[0],),
        far=(0, 1, 2),
        limit=4,
        scratch=[
            pltpu.VMEM(context.shape, context.dtype),
            pltpu.VMEM(out_grad.shape, out_grad.dtype),
            pltpu.VMEM(kept_rows.shape, kept_rows.dtype),
            dma((3,)),
        ],
    )[0]
    route = call(
        route_kernel, "route", (ids, probs), [shape(3, token_count, 384)], after=(partial,)
    )[0]
    own, other = call(
        split_kernel, "split", tuple(arrived), [shape(ROWS, columns)] * 2, after=(route,)
    )
    own_far = swap(own, "tensor", 1)
    crossed = swap(other, "tensor", 2)

    def hold(value, *after):
        return call(pass_kernel, "hold", (value,), [value], after=after, aliases={0: 0})[0]

    held = hold(partial, own)
    begun = call(
        begun_kernel, "begun", (own, gate_weight, up_weight), [shape(ROWS, CHUNKS[0], dtype=f32)] * 2
    )
    crossed = hold(crossed, begun[0])
    crossed_far = swap(crossed, "tensor", 1)
    pieces = (own, own_far, crossed, crossed_far)

    hidden, remote, last = [], [], route
    for k, width in enumerate(CHUNKS):
        made = call(
            functools.partial(hidden_kernel, STARTS[k]),
            "hidden",
            (*pieces, *(begun if k == 0 else ()), gate_weight, up_weight),
            [shape(ROWS, width), shape(REMOTE, width)],
            after=(last,),
            cost=20 if k == 0 else 0,
        )
        hidden.append(made[0])
        remote.append(made[1])
        last = made[0]
        if k == 1:
            last = pair = call(
                sum_kernel, "pair_sum", (held, swap(held, "rank", 1)), [shape(*blocks)], after=(last,)
            )[0]
    across = [swap(part, "tensor", 2) for part in remote]
    *full, own_rows = call(
        merge_kernel,
        "merge",
        tuple(hidden),
        [shape(ROWS, HALF // 2)] * 2 + [shape(MOST, HALF)],
    )
    full_far = [swap(part, "tensor", 1) for part in full]
    own_across = swap(own_rows, "tensor", 2)

    def add(pieces, parts, total, after=()):
        rows = parts[0].shape[0]
        operands = (*parts, down_weight) + (() if total is None else (total,))
        return call(
            functools.partial(down_add_kernel, pieces, total is not None),
            "down_add",
            operands,
            [shape(rows, columns, dtype=f32)],
            after=after,
        )[0]

    total, step = None, own_rows
    fars = []
    for k, start in enumerate(STARTS):
        if k == 1:
            masked_grad, step = call(
                masked_sum_kernel,
                "masked_sum",
                (pair, swap(pair, "rank", 2)),
                [shape(*blocks, dtype=f32), shape(8, 128, dtype=f32)],
                after=(total,),
            )
        if k == 2:
            mine = call(
                functools.partial(down_add_kernel, OWN_NEAR, False),
                "down_add",
                (*full, down_weight),
                [shape(ROWS, columns, dtype=f32)],
                after=(total,),
            )[0]
            step = mine
        near = hold(across[k], step)
        far = swap(near, "tensor", 1)
        total = add(((start, 1, 0),), (near,), total)
        fars.append(((start, 1, 1), far))
        for j in FLUSH[k]:
            total = add((fars[j][0],), (fars[j][1],), total)
        step = total
    mine = add(OWN_FAR, full_far, mine, (total,))
    *backs, own = call(
        back_kernel,
        "back",
        (total, mine),
        [shape(2 * MOST, columns)] * 3 + [shape(MOST, columns)],
    )
    back = {s: swap(backs[s - 1], "rank", s) for s in SEND_ORDER}
    lists = [back[s] for s in (1, 2, 3)]
    near = hold(own_across, *reversed(lists))
    far = swap(near, "tensor", 1)
    last = add(((0, 1, 0),), (near,), None)
    last = add(((0, 1, 1),), (far,), last)
    layer_output, router = call(
        combine_kernel,
        "combine",
        (own, last, *reversed(lists), route, out_grad),
        [shape(token_count, columns), shape(8, token_count, dtype=f32)],
    )
    scores = {t: swap(router, "tensor", t) for t in (2, 3, 1)}
    routers = [router] + [scores[t] for t in (1, 2, 3)]
    router_grad = call(router_kernel, "router", tuple(routers), [shape(2, token_count, dtype=f32)])[0]
    return (layer_output, router_grad.T, masked_grad)


def solution(mesh):
    ranks, tensors = mesh.shape["rank"], mesh.shape["tensor"]
    body = routed if (ranks, tensors) == (4, 4) else shards
    return jax.shard_map(
        body,
        mesh=mesh,
        in_specs=(
            P(("groups", "rank"), "tensor"),
            P(("groups", "rank"), "tensor"),
            P(("groups", "rank"), None),
            P(("groups", "rank"), None),
            P(("groups", "rank"), None),
            P(None, ("rank", "tensor")),
            P(None, ("rank", "tensor")),
            P("rank", "tensor"),
            P("tensor", None),
        ),
        out_specs=(
            P(("groups", "rank"), "tensor"),
            P(("groups", "rank"), None),
            P(("groups", "tensor"), None, None),
        ),
        check_vma=False,
    )
```
